32 devices in a mesh: group: 2 (over x), band: 16 (over z, y, core).
Axes of the slice: x: 2, y: 2, z: 4, core: 2. Of those that a mesh axis runs over, the one named last changes fastest.
Arguments:
- samples: bfloat16 [16384, 2, 4096], P(('group', 'band')), parts along dimension 0, may hold values from -6 to 6
- channel_delay: int32 [8192, 128], P('band'), may hold values from 0 to 15
- merge_rows: int32 [4, 2, 2048], P(None, None, 'band'), may hold values from 0 to 127
- merge_shift: int32 [4, 2048], P(None, 'band'), may hold values from 0 to 63
- destination: int32 [2048], P('band'), may hold values from 0 to 2047, as said below
- widths: int32 [2048], P('band'), may hold values from 1 to 64
Outputs:
- filtered: float32 [4096, 2, 3584], P(('group', 'band')), parts along dimension 0
The draws below stay inside these ranges and needn't reach their ends.
There are 2 independent parts, one for each index of `group`. The reference program is written for one: setup_inputs(seed, part) draws one part's arguments, and reference() takes and returns one part's arrays. A program takes and returns all parts, laid end to end along the dimension named above; an argument that names none is the same for every part. Nothing has to cross between parts.
Inputs may be any that keep to these rules, and one draw needn't show every extreme that they name: destination is a permutation of the trials; the 128 trials of each band go 8 to each owner block of 128 positions, and those of band k land at positions k * 8 to (k + 1) * 8 - 1 of that block.
All inputs are finite; a program needn't handle non-finite values.
Results may differ from the reference program's by a relative error of at most 0.0064.
Values may be sent and summed in bfloat16 or wider, within the bound.
A program may use at most 192 MiB of HBM per device.

```python
import math
import jax
import jax.numpy as jnp
from jax import lax

CH_DEV = 512
R = 128
FL = 4096
DL = 16
DM = 64
WMAX = 64
NSLAB = 2
VALID = 3584
LEVELS = 4
CHANNELS = 8192
TRIALS = 2048
N_BAND = 16


def draw_destination(key, part):
    key = jax.random.fold_in(key, 7)
    blocks_count = TRIALS // R
    share = R // blocks_count
    keys = jax.random.split(key, blocks_count)
    orders = jax.vmap(lambda one_key: jax.random.permutation(one_key, R))(keys).astype(jnp.int32)
    owner = orders // share
    slot_index = jnp.arange(blocks_count, dtype=jnp.int32)[:, None] * share + orders % share
    return (owner * R + slot_index).reshape(TRIALS).astype(jnp.int32)


def with_ends(drawn, own_key, least, high):
    place = [jax.random.randint(jax.random.fold_in(own_key, axis), (), 0, length) for axis, length in enumerate(drawn.shape)]
    widest = drawn.shape.index(max(drawn.shape))
    next_to = place[:widest] + [(place[widest] + 1) % drawn.shape[widest]] + place[widest + 1:]
    return drawn.at[tuple(place)].set(least).at[tuple(next_to)].set(high)


def shard_levels(key, shape, cuts, smallest, high):
    gain, own = 1.0, jax.random.fold_in(key, 6)
    for dim, blocks in cuts:
        heights = jnp.exp(jax.random.uniform(jax.random.fold_in(own, dim), (blocks,), jnp.float32, smallest / len(cuts), high / len(cuts)))
        gain = gain * jnp.repeat(heights, shape[dim] // blocks).reshape([-1 if axis == dim else 1 for axis in range(len(shape))])
    return gain


def centred(stream_key, shape, spread, limit, cuts=(), kind=jnp.bfloat16):
    values = jax.random.normal(stream_key, shape, jnp.float32) * spread
    if len(cuts) > 0:
        values = shard_levels(stream_key, shape, cuts, -0.22, 0.18) * values
    return jnp.clip(values, min=-limit, max=limit).astype(kind)


def setup_inputs(seed: int = 0, part: int = 0) -> dict:
    key_list = jax.random.split(jax.random.key(seed), 7)
    part_keys = jax.random.split(jax.random.fold_in(key_list[6], part), 7)
    samples = centred(part_keys[0], (CHANNELS, NSLAB, FL), 1.0, 6.0, ((0, 16),))
    channel_delay = with_ends(jax.random.randint(key_list[1], (CHANNELS, R), 0, DL), jax.random.fold_in(key_list[1], 1), 0, DL - 1).astype(jnp.int32)
    merge_rows = with_ends(jax.random.randint(key_list[2], (LEVELS, 2, TRIALS), 0, R), jax.random.fold_in(key_list[2], 1), 0, R - 1).astype(jnp.int32)
    merge_shift = with_ends(jax.random.randint(key_list[3], (LEVELS, TRIALS), 0, DM), jax.random.fold_in(key_list[3], 1), 0, DM - 1).astype(jnp.int32)
    destination = draw_destination(jax.random.fold_in(key_list[6], 71), part)
    widths = with_ends(jax.random.randint(key_list[5], (TRIALS,), 1, WMAX + 1), jax.random.fold_in(key_list[5], 1), 1, WMAX).astype(jnp.int32)
    return dict(samples=samples, channel_delay=channel_delay, merge_rows=merge_rows, merge_shift=merge_shift, destination=destination, widths=widths)


half_root = 0.7071067811865476

def local_tree(block_samples, block_delay):
    summed = jnp.zeros((R, NSLAB, FL), jnp.float32)
    samples_wide = block_samples.astype(jnp.float32)
    for delay_value in range(DL):
        select = (block_delay == delay_value).astype(jnp.float32)
        product = jnp.einsum('cr,csf->rsf', select, samples_wide)
        if delay_value:
            product = jnp.pad(product[:, :, delay_value:], ((0, 0), (0, 0), (0, delay_value)))
        summed = summed + product
    return (summed * (1.0 / math.sqrt(CH_DEV))).astype(jnp.bfloat16)

def shift_row(row_data, amount):
    padded = jnp.pad(row_data, ((0, 0), (0, DM)))
    return lax.dynamic_slice_in_dim(padded, amount.astype(jnp.int32), FL, axis=1)

def reference(samples, channel_delay, merge_rows, merge_shift, destination, widths):
    samples_blocks = samples.reshape(N_BAND, CH_DEV, NSLAB, FL)
    delay_blocks = channel_delay.reshape(N_BAND, CH_DEV, R)
    current = lax.map(lambda pair_args: local_tree(pair_args[0], pair_args[1]), (samples_blocks, delay_blocks))
    band_ids = jnp.arange(N_BAND, dtype=jnp.int32)
    for level_index in range(LEVELS):
        bit_value = 1 << level_index
        low_ids = band_ids - jnp.bitwise_and(band_ids, bit_value)
        high_ids = jnp.bitwise_or(band_ids, bit_value)
        low_blocks = current[low_ids]
        high_blocks = current[high_ids]
        low_index = merge_rows[level_index, 0].reshape(N_BAND, R)
        high_index = merge_rows[level_index, 1].reshape(N_BAND, R)
        shift_amounts = merge_shift[level_index].reshape(N_BAND, R)
        low_pick = jax.vmap(lambda blk_rows, picks: jnp.take(blk_rows, picks, axis=0))(low_blocks, low_index)
        high_pick = jax.vmap(lambda blk_rows, picks: jnp.take(blk_rows, picks, axis=0))(high_blocks, high_index)
        moved = jax.vmap(jax.vmap(shift_row))(high_pick, shift_amounts)
        current = ((low_pick.astype(jnp.float32) + moved.astype(jnp.float32)) * half_root).astype(jnp.bfloat16)
    dedispersed = current.reshape(TRIALS, NSLAB, FL)
    regrouped = jnp.zeros_like(dedispersed).at[destination].set(dedispersed)
    width_float = widths.astype(jnp.float32)
    boxcar = jnp.where(jnp.arange(FL, dtype=jnp.int32)[None, :] < widths[:, None], (1.0 / jnp.sqrt(width_float))[:, None], jnp.zeros((), jnp.float32))
    kernel_spec = jnp.fft.fft(boxcar, axis=-1)
    data_spec = jnp.fft.fft(regrouped.astype(jnp.float32), axis=-1)
    result = jnp.fft.ifft(data_spec * jnp.conj(kernel_spec)[:, None, :], axis=-1).real
    return result[:, :, :VALID].astype(jnp.float32)
```

```python
import functools
import math

import jax
import jax.numpy as jnp
from jax import lax
from jax.experimental import pallas as pl
from jax.experimental.pallas import tpu as pltpu
from jax.sharding import PartitionSpec as P

MARGIN = 512
DL = 16
DM = 64
LANES = 128
SUBLANES = 8
GROUP = 16
half_root = 0.7071067811865476
f32 = jnp.float32
bf16 = jnp.bfloat16
VMEM_BYTES = 58 * 2**20


def level0_kernel(chunks, chunk, halo, delay_ref, x_ref, next_ref, out_ref, sel_ref):
    slab = pl.program_id(0)
    piece = pl.program_id(1)
    rows = delay_ref.shape[0]
    channels = delay_ref.shape[1]

    @pl.when((slab == 0) & (piece == 0))
    def _():
        for d in range(DL):
            sel_ref[d * rows : (d + 1) * rows, :] = jnp.where(
                delay_ref[...] == d, 1.0, 0.0
            ).astype(bf16)

    alive = jnp.where(piece + 1 < chunks, 1.0, 0.0).astype(bf16)
    x = jnp.concatenate([x_ref[0], next_ref[0] * alive], axis=1)
    total = jnp.zeros((rows, chunk), f32)
    per = 4
    for first in range(0, DL, per):
        y = jnp.dot(
            sel_ref[first * rows : (first + per) * rows, :], x, preferred_element_type=f32
        )
        for d in range(first, first + per):
            part = y[(d - first) * rows : (d - first + 1) * rows, :]
            total = total + part[:, d : d + chunk]
    value = (total * (1.0 / math.sqrt(channels))).astype(bf16)
    here = slab * chunks + piece
    out_ref[pl.ds(here, 1), :, 0:chunk] = value[None]
    reach = -(-halo // chunk)
    for back in range(1, reach + 1):
        stop = min((back + 1) * chunk, chunk + halo)
        width = stop - back * chunk

        @pl.when(piece >= back)
        def _():
            out_ref[pl.ds(here - back, 1), :, back * chunk : stop] = value[None, :, :width]

        @pl.when(piece + back >= chunks)
        def _():
            out_ref[pl.ds(here, 1), :, back * chunk : stop] = jnp.zeros((1, rows, width), bf16)


def level0(samples, channel_delay, parts, halo):
    slabs, channels, length = samples.shape
    rows = channel_delay.shape[1]
    chunks = parts // slabs
    chunk = length // chunks
    tiles = chunk // LANES
    last = length // LANES - 1
    return pl.pallas_call(
        functools.partial(level0_kernel, chunks, chunk, halo),
        grid=(slabs, chunks),
        in_specs=[
            pl.BlockSpec((rows, channels), lambda s, c: (0, 0)),
            pl.BlockSpec((1, channels, chunk), lambda s, c: (s, 0, c)),
            pl.BlockSpec(
                (1, channels, LANES), lambda s, c: (s, 0, jnp.minimum((c + 1) * tiles, last))
            ),
        ],
        out_specs=pl.BlockSpec((parts, rows, chunk + halo), lambda s, c: (0, 0, 0)),
        out_shape=jax.ShapeDtypeStruct((parts, rows, chunk + halo), bf16),
        scratch_shapes=[pltpu.VMEM((DL * rows, channels), bf16)],
        compiler_params=pltpu.CompilerParams(vmem_limit_bytes=VMEM_BYTES),
        name="level0",
    )(channel_delay.T, samples, samples)


def tree_kernel(levels, keep, table_ref, dest_ref, x_ref, out_ref, a_ref, b_ref, o_ref):
    trials, extent = x_ref.shape
    rows = out_ref.shape[1]

    def stage(g, carry):
        x = x_ref[pl.ds(pl.multiple_of(g * GROUP, GROUP), GROUP), :].astype(f32)
        for j in range(SUBLANES):
            if j * LANES < extent:
                piece = x[:, j * LANES : (j + 1) * LANES]
            else:
                piece = jnp.zeros((GROUP, LANES), f32)
            a_ref[pl.ds(g * GROUP * SUBLANES + j, GROUP, stride=SUBLANES), :] = piece
        return carry

    lax.fori_loop(0, trials // GROUP, stage, 0)
    lane = lax.broadcasted_iota(jnp.int32, (SUBLANES, LANES), 1)
    for level in range(levels):
        src, dst = (a_ref, b_ref) if level % 2 == 0 else (b_ref, a_ref)

        def merge(g, carry):
            values = []
            for i in range(GROUP):
                word = table_ref[level, g * GROUP + i]
                low = jnp.bitwise_and(word, 4095)
                high = jnp.bitwise_and(jnp.right_shift(word, 12), 4095)
                shift = jnp.right_shift(word, 24)
                v_low = src[pl.ds(pl.multiple_of(low * SUBLANES, SUBLANES), SUBLANES), :]
                v_high = src[pl.ds(pl.multiple_of(high * SUBLANES, SUBLANES), SUBLANES), :]
                turned = pltpu.roll(v_high, jnp.bitwise_and(LANES - shift, LANES - 1), 1)
                after = pltpu.roll(turned, SUBLANES - 1, 0)
                moved = jnp.where(lane < LANES - shift, turned, after)
                values.append(((v_low + moved) * half_root).astype(bf16).astype(f32))
            for i in range(GROUP):
                q = g * GROUP + i
                if level + 1 < levels:
                    dst[pl.ds(pl.multiple_of(q * SUBLANES, SUBLANES), SUBLANES), :] = values[i]
                else:
                    o_ref[pl.ds(dest_ref[q], keep, stride=rows), :] = values[i][:keep]
            return carry

        lax.fori_loop(0, trials // GROUP, merge, 0)

    def pack(g, carry):
        out_ref[g] = o_ref[pl.ds(pl.multiple_of(g * rows, rows), rows), :].astype(bf16)
        return carry

    lax.fori_loop(0, out_ref.shape[0], pack, 0)


def tree(table, places, arrived, keep, rows):
    levels = table.shape[0]
    trials = arrived.shape[0]
    blocks = trials // rows * keep
    whole = pl.BlockSpec(memory_space=pltpu.VMEM)
    scalars = pl.BlockSpec(memory_space=pltpu.SMEM)
    return pl.pallas_call(
        functools.partial(tree_kernel, levels, keep),
        in_specs=[scalars, scalars, whole],
        out_specs=whole,
        out_shape=jax.ShapeDtypeStruct((blocks, rows, LANES), bf16),
        scratch_shapes=[
            pltpu.VMEM((trials * SUBLANES, LANES), f32),
            pltpu.VMEM((trials * SUBLANES, LANES), f32),
            pltpu.VMEM((blocks * rows, LANES), f32),
        ],
        compiler_params=pltpu.CompilerParams(vmem_limit_bytes=VMEM_BYTES),
        name="tree",
    )(table, places, arrived)


PITCH = 40


def boxcar_kernel(slabs, valid, widths_ref, scales_ref, x_ref, out_ref, p_ref, t_ref):
    blocks, rows, _ = x_ref.shape
    per_slab = blocks // slabs
    row = lax.broadcasted_iota(jnp.int32, (LANES, 2 * LANES), 0)
    col = lax.broadcasted_iota(jnp.int32, (LANES, 2 * LANES), 1)
    sums = jnp.where(row < col, 1.0, 0.0).astype(bf16)

    def prefix(i, carry):
        for s in range(slabs):
            y = jnp.dot(x_ref[s * per_slab + i], sums, preferred_element_type=f32)
            p_ref[pl.ds(s * rows * PITCH + i, rows, stride=PITCH), :] = y[:, :LANES]
            t_ref[pl.ds(s * rows * PITCH + i, rows, stride=PITCH), :] = y[:, LANES:]
        return carry

    lax.fori_loop(0, valid + 1, prefix, 0)
    lane = lax.broadcasted_iota(jnp.int32, (SUBLANES, LANES), 1)

    def window(g, carry):
        for i in range(2):
            p = g * 2 + i
            width = widths_ref[p]
            scale = scales_ref[p]
            amount = LANES - width
            for s in range(slabs):
                base = pl.multiple_of((s * rows + p) * PITCH, SUBLANES)
                for b in range(0, valid, SUBLANES):
                    here = p_ref[pl.ds(base + b, SUBLANES), :]
                    after = p_ref[pl.ds(base + b + 1, SUBLANES), :]
                    whole = t_ref[pl.ds(base + b, SUBLANES), :]
                    end = jnp.where(
                        lane < amount,
                        pltpu.roll(here, amount, 1),
                        pltpu.roll(after, amount, 1) + whole,
                    )
                    value = (end - here) * scale
                    count = min(SUBLANES, valid - b)
                    out_ref[pl.ds(p * (valid * slabs) + b * slabs + s, count, stride=slabs), :] = value[:count]
        return carry

    lax.fori_loop(0, rows // 2, window, 0)


def boxcar(widths, arrived, slabs, valid):
    rows = arrived.shape[1]
    whole = pl.BlockSpec(memory_space=pltpu.VMEM)
    scalars = pl.BlockSpec(memory_space=pltpu.SMEM)
    return pl.pallas_call(
        functools.partial(boxcar_kernel, slabs, valid),
        in_specs=[scalars, scalars, whole],
        out_specs=whole,
        out_shape=jax.ShapeDtypeStruct((rows * valid * slabs, LANES), f32),
        scratch_shapes=[
            pltpu.VMEM((slabs * rows * PITCH, LANES), f32),
            pltpu.VMEM((slabs * rows * PITCH, LANES), f32),
        ],
        compiler_params=pltpu.CompilerParams(vmem_limit_bytes=VMEM_BYTES),
        name="boxcar",
    )(widths, 1.0 / jnp.sqrt(widths.astype(f32)), arrived)


def body(samples, channel_delay, merge_rows, merge_shift, destination, widths):
    slabs, length = samples.shape[1], samples.shape[2]
    rows = channel_delay.shape[1]
    parts = lax.axis_size("band")
    levels = merge_shift.shape[0]
    position = lax.axis_index("band")
    chunk = slabs * length // parts
    keep = chunk // LANES
    halo = -(-levels * (DM - 1) // LANES) * LANES

    bits = (2 ** jnp.arange(levels, dtype=jnp.int32))[:, None]
    low = (position & ~bits) * rows + merge_rows[:, 0]
    high = (position | bits) * rows + merge_rows[:, 1]
    owner, slot = destination // rows, destination % rows
    place = owner * (keep * rows) + slot
    tables = jnp.concatenate([low, high, merge_shift, place[None]], axis=0)
    tables = lax.all_gather(tables, "band", axis=1, tiled=True)
    table = (
        tables[:levels]
        + tables[levels : 2 * levels] * 4096
        + tables[2 * levels : 3 * levels] * (4096 * 4096)
    )
    places = tables[3 * levels]

    outgoing = level0(jnp.transpose(samples, (1, 0, 2)), channel_delay, parts, halo)
    arrived = lax.all_to_all(outgoing, "band", split_axis=0, concat_axis=0, tiled=True)
    merged = tree(table, places, arrived.reshape(parts * rows, chunk + halo), keep, rows)
    grouped = lax.all_to_all(merged, "band", split_axis=0, concat_axis=0, tiled=True)
    valid = (length - MARGIN) // LANES
    result = boxcar(widths, grouped, slabs, valid)
    result = result.reshape(rows, valid, slabs, LANES).transpose(0, 2, 1, 3)
    return result.reshape(rows, slabs, valid * LANES)


def solution(mesh):
    return jax.shard_map(
        body,
        mesh=mesh,
        in_specs=(
            P(("group", "band"), None, None),
            P("band", None),
            P(None, None, "band"),
            P(None, "band"),
            P("band"),
            P("band"),
        ),
        out_specs=P(("group", "band"), None, None),
        check_vma=False,
    )
```

```python
import functools
import math

import jax
import jax.numpy as jnp
from jax import lax
from jax.experimental import pallas as pl
from jax.experimental.pallas import tpu as pltpu
from jax.sharding import PartitionSpec as P

MARGIN = 512
DL = 16
DM = 64
LANES = 128
SUBLANES = 8
GROUP = 16
UNROLL = 64
SPLITS = 2
half_root = 0.7071067811865476
f32 = jnp.float32
bf16 = jnp.bfloat16
VMEM_BYTES = 58 * 2**20


def level0_kernel(span, chunks, chunk, halo, delay_ref, x_ref, next_ref, out_ref, sel_ref):
    slab = pl.program_id(0)
    piece = pl.program_id(1)
    rows = delay_ref.shape[0]
    channels = delay_ref.shape[1]

    @pl.when((slab == 0) & (piece == 0))
    def _():
        for d in range(DL):
            sel_ref[d * rows : (d + 1) * rows, :] = jnp.where(
                delay_ref[...] == d, 1.0, 0.0
            ).astype(bf16)

    alive = jnp.where((piece + 1) * span < chunks, 1.0, 0.0).astype(bf16)
    x = jnp.concatenate([x_ref[0], next_ref[0] * alive], axis=1)
    total = jnp.zeros((rows, chunk * span), f32)
    per = 4
    for first in range(0, DL, per):
        y = jnp.dot(
            sel_ref[first * rows : (first + per) * rows, :], x, preferred_element_type=f32
        )
        for d in range(first, first + per):
            part = y[(d - first) * rows : (d - first + 1) * rows, :]
            total = total + part[:, d : d + chunk * span]
    value = (total * (1.0 / math.sqrt(channels))).astype(bf16)
    reach = -(-halo // chunk)
    for k in range(span):
        own = value[None, :, k * chunk : (k + 1) * chunk]
        index = piece * span + k
        here = slab * chunks + index
        out_ref[pl.ds(here, 1), :, 0:chunk] = own
        for back in range(1, reach + 1):
            stop = min((back + 1) * chunk, chunk + halo)
            width = stop - back * chunk

            @pl.when(index >= back)
            def _():
                out_ref[pl.ds(here - back, 1), :, back * chunk : stop] = own[:, :, :width]

            @pl.when(index + back >= chunks)
            def _():
                out_ref[pl.ds(here, 1), :, back * chunk : stop] = jnp.zeros((1, rows, width), bf16)


def level0(samples, channel_delay, parts, halo):
    slabs, channels, length = samples.shape
    rows = channel_delay.shape[1]
    chunks = parts // slabs
    chunk = length // chunks
    span = 2 if chunks % 2 == 0 else 1
    tiles = span * chunk // LANES
    last = length // LANES - 1
    return pl.pallas_call(
        functools.partial(level0_kernel, span, chunks, chunk, halo),
        grid=(slabs, chunks // span),
        in_specs=[
            pl.BlockSpec((rows, channels), lambda s, c: (0, 0)),
            pl.BlockSpec((1, channels, chunk * span), lambda s, c: (s, 0, c)),
            pl.BlockSpec(
                (1, channels, LANES), lambda s, c: (s, 0, jnp.minimum((c + 1) * tiles, last))
            ),
        ],
        out_specs=pl.BlockSpec((parts, rows, chunk + halo), lambda s, c: (0, 0, 0)),
        out_shape=jax.ShapeDtypeStruct((parts, rows, chunk + halo), bf16),
        scratch_shapes=[pltpu.VMEM((DL * rows, channels), bf16)],
        compiler_params=pltpu.CompilerParams(vmem_limit_bytes=VMEM_BYTES),
        name="level0",
    )(channel_delay.T, samples, samples)


def tree_kernel(levels, keep, low_ref, high_ref, amount_ref, dest_ref, *refs):
    x_refs, (out_ref, a_ref, b_ref, o_ref) = refs[:-4], refs[-4:]
    extent = x_refs[0].shape[1]
    rows = out_ref.shape[1]
    trials = low_ref.shape[1]
    cut = rows // len(x_refs)

    def stage(k, carry):
        for half, x_ref in enumerate(x_refs):
            for g in range(0, cut, GROUP):
                x = x_ref[pl.ds(pl.multiple_of(k * cut, GROUP) + g, GROUP), :].astype(f32)
                first = (k * rows + half * cut + g) * SUBLANES
                for j in range(SUBLANES):
                    if j * LANES < extent:
                        piece = x[:, j * LANES : (j + 1) * LANES]
                    else:
                        piece = jnp.zeros((GROUP, LANES), f32)
                    a_ref[pl.ds(first + j, GROUP, stride=SUBLANES), :] = piece
        return carry

    lax.fori_loop(0, trials // rows, stage, 0)
    lane = lax.broadcasted_iota(jnp.int32, (SUBLANES, LANES), 1)
    for level in range(levels):
        src, dst = (a_ref, b_ref) if level % 2 == 0 else (b_ref, a_ref)

        def merge(g, carry):
            for i in range(UNROLL):
                q = g * UNROLL + i
                low = pl.multiple_of(low_ref[level, q], SUBLANES)
                high = pl.multiple_of(high_ref[level, q], SUBLANES)
                amount = amount_ref[level, q]
                v_low = src[pl.ds(low, SUBLANES), :]
                v_high = src[pl.ds(high, SUBLANES), :]
                turned = pltpu.roll(v_high, amount, 1)
                after = pltpu.roll(turned, SUBLANES - 1, 0)
                moved = jnp.where(lane < amount, turned, after)
                value = ((v_low + moved) * half_root).astype(bf16).astype(f32)
                if level + 1 < levels:
                    dst[pl.ds(pl.multiple_of(q * SUBLANES, SUBLANES), SUBLANES), :] = value
                else:
                    o_ref[pl.ds(dest_ref[q], keep, stride=rows), :] = value[:keep]
            return carry

        lax.fori_loop(0, trials // UNROLL, merge, 0)

    def pack(g, carry):
        out_ref[g] = o_ref[pl.ds(pl.multiple_of(g * rows, rows), rows), :].astype(bf16)
        return carry

    lax.fori_loop(0, out_ref.shape[0], pack, 0)


def tree(low, high, amount, places, arrived, keep, rows):
    levels = low.shape[0]
    trials = low.shape[1]
    blocks = trials // rows * keep
    whole = pl.BlockSpec(memory_space=pltpu.VMEM)
    scalars = pl.BlockSpec(memory_space=pltpu.SMEM)
    return pl.pallas_call(
        functools.partial(tree_kernel, levels, keep),
        in_specs=[scalars] * 4 + [whole] * len(arrived),
        out_specs=whole,
        out_shape=jax.ShapeDtypeStruct((blocks, rows, LANES), bf16),
        scratch_shapes=[
            pltpu.VMEM((trials * SUBLANES, LANES), f32),
            pltpu.VMEM((trials * SUBLANES, LANES), f32),
            pltpu.VMEM((blocks * rows, LANES), f32),
        ],
        compiler_params=pltpu.CompilerParams(vmem_limit_bytes=VMEM_BYTES),
        name="tree",
    )(low, high, amount, places, *arrived)


def boxcar_kernel(valid, pitch, widths_ref, scales_ref, x_ref, out_ref, p_ref, t_ref):
    blocks, rows, _ = x_ref.shape
    slabs = out_ref.shape[1]
    per_slab = blocks // slabs
    row = lax.broadcasted_iota(jnp.int32, (LANES, 2 * LANES), 0)
    col = lax.broadcasted_iota(jnp.int32, (LANES, 2 * LANES), 1)
    sums = jnp.where(row < col, 1.0, 0.0).astype(bf16)

    for i in range(valid + 1):
        for s in range(slabs):
            y = jnp.dot(x_ref[s * per_slab + i], sums, preferred_element_type=f32)
            p_ref[pl.ds(i * slabs + s, rows, stride=pitch), :] = y[:, :LANES]
            t_ref[pl.ds(i * slabs + s, rows, stride=pitch), :] = y[:, LANES:]
    lane = lax.broadcasted_iota(jnp.int32, (SUBLANES, LANES), 1)

    def window(g, carry):
        for i in range(4):
            p = g * 4 + i
            scale = scales_ref[p]
            amount = LANES - widths_ref[p]
            base = pl.multiple_of(p * pitch, SUBLANES)
            for b in range(0, valid * slabs, SUBLANES):
                here = p_ref[pl.ds(base + b, SUBLANES), :]
                after = p_ref[pl.ds(base + b + slabs, SUBLANES), :]
                whole = t_ref[pl.ds(base + b, SUBLANES), :]
                end = jnp.where(
                    lane < amount,
                    pltpu.roll(here, amount, 1),
                    pltpu.roll(after, amount, 1) + whole,
                )
                value = (end - here) * scale
                for j in range(0, min(SUBLANES, valid * slabs - b), slabs):
                    t = (b + j) // slabs
                    out_ref[p, :, t * LANES : (t + 1) * LANES] = value[j : j + slabs]
        return carry

    lax.fori_loop(0, rows // 4, window, 0)


def boxcar(widths, arrived, slabs, valid):
    rows = arrived.shape[1]
    pitch = -(-(valid + 1) * slabs // SUBLANES) * SUBLANES + SUBLANES
    whole = pl.BlockSpec(memory_space=pltpu.VMEM)
    scalars = pl.BlockSpec(memory_space=pltpu.SMEM)
    return pl.pallas_call(
        functools.partial(boxcar_kernel, valid, pitch),
        in_specs=[scalars, scalars, whole],
        out_specs=whole,
        out_shape=jax.ShapeDtypeStruct((rows, slabs, valid * LANES), f32),
        scratch_shapes=[
            pltpu.VMEM((rows * pitch, LANES), f32),
            pltpu.VMEM((rows * pitch, LANES), f32),
        ],
        compiler_params=pltpu.CompilerParams(vmem_limit_bytes=VMEM_BYTES),
        name="boxcar",
    )(widths, 1.0 / jnp.sqrt(widths.astype(f32)), arrived)


def body(samples, channel_delay, merge_rows, merge_shift, destination, widths):
    slabs, length = samples.shape[1], samples.shape[2]
    rows = channel_delay.shape[1]
    parts = lax.axis_size("band")
    levels = merge_shift.shape[0]
    position = lax.axis_index("band")
    chunk = slabs * length // parts
    keep = chunk // LANES
    halo = -(-levels * (DM - 1) // LANES) * LANES

    bits = (2 ** jnp.arange(levels, dtype=jnp.int32))[:, None]
    low = (position & ~bits) * rows + merge_rows[:, 0]
    high = (position | bits) * rows + merge_rows[:, 1]
    owner, slot = destination // rows, destination % rows
    place = owner * (keep * rows) + slot
    tables = jnp.concatenate([low, high, merge_shift, place[None]], axis=0)
    by_slab = jnp.transpose(samples, (1, 0, 2))
    arrived = []
    cut = rows // SPLITS
    for i in range(SPLITS):
        outgoing = level0(by_slab, channel_delay[:, i * cut : (i + 1) * cut], parts, halo)
        block = lax.all_to_all(outgoing, "band", split_axis=0, concat_axis=0, tiled=True)
        arrived.append(block.reshape(parts * cut, chunk + halo))
        if i == 0:
            arrived[0], tables = lax.optimization_barrier((arrived[0], tables))
    tables = lax.all_gather(tables, "band", axis=1, tiled=True)
    low = tables[:levels] * SUBLANES
    high = tables[levels : 2 * levels] * SUBLANES
    amount = LANES - tables[2 * levels : 3 * levels]
    places = tables[3 * levels]
    merged = tree(low, high, amount, places, arrived, keep, rows)
    grouped = lax.all_to_all(merged, "band", split_axis=0, concat_axis=0, tiled=True)
    valid = (length - MARGIN) // LANES
    return boxcar(widths, grouped, slabs, valid)


def solution(mesh):
    return jax.shard_map(
        body,
        mesh=mesh,
        in_specs=(
            P(("group", "band"), None, None),
            P("band", None),
            P(None, None, "band"),
            P(None, "band"),
            P("band"),
            P("band"),
        ),
        out_specs=P(("group", "band"), None, None),
        check_vma=False,
    )
```

```python
import functools
import math

import jax
import jax.numpy as jnp
from jax import lax
from jax.experimental import pallas as pl
from jax.experimental.pallas import tpu as pltpu
from jax.sharding import PartitionSpec as P

MARGIN = 512
DL = 16
DM = 64
LANES = 128
SUBLANES = 8
GROUP = 16
UNROLL = 128
half_root = 0.7071067811865476
f32 = jnp.float32
bf16 = jnp.bfloat16
VMEM_BYTES = 58 * 2**20


def level0_kernel(span, chunks, chunk, halo, delay_ref, x_ref, next_ref, out_ref, sel_ref):
    slab = pl.program_id(0)
    piece = pl.program_id(1)
    rows = delay_ref.shape[0]
    channels = delay_ref.shape[1]

    @pl.when((slab == 0) & (piece == 0))
    def _():
        for d in range(DL):
            sel_ref[d * rows : (d + 1) * rows, :] = jnp.where(
                delay_ref[...] == d, 1.0, 0.0
            ).astype(bf16)

    alive = jnp.where((piece + 1) * span < chunks, 1.0, 0.0).astype(bf16)
    x = jnp.concatenate([x_ref[0], next_ref[0] * alive], axis=1)
    total = jnp.zeros((rows, chunk * span), f32)
    per = 4
    for first in range(0, DL, per):
        y = jnp.dot(
            sel_ref[first * rows : (first + per) * rows, :], x, preferred_element_type=f32
        )
        for d in range(first, first + per):
            part = y[(d - first) * rows : (d - first + 1) * rows, :]
            total = total + part[:, d : d + chunk * span]
    value = (total * (1.0 / math.sqrt(channels))).astype(bf16)
    reach = -(-halo // chunk)
    for k in range(span):
        own = value[None, :, k * chunk : (k + 1) * chunk]
        index = piece * span + k
        here = slab * chunks + index
        out_ref[pl.ds(here, 1), :, 0:chunk] = own
        for back in range(1, reach + 1):
            stop = min((back + 1) * chunk, chunk + halo)
            width = stop - back * chunk

            @pl.when(index >= back)
            def _():
                out_ref[pl.ds(here - back, 1), :, back * chunk : stop] = own[:, :, :width]

            @pl.when(index + back >= chunks)
            def _():
                out_ref[pl.ds(here, 1), :, back * chunk : stop] = jnp.zeros((1, rows, width), bf16)


def level0(samples, channel_delay, parts, halo):
    slabs, channels, length = samples.shape
    rows = channel_delay.shape[1]
    chunks = parts // slabs
    chunk = length // chunks
    span = 2 if chunks % 2 == 0 else 1
    tiles = span * chunk // LANES
    last = length // LANES - 1
    return pl.pallas_call(
        functools.partial(level0_kernel, span, chunks, chunk, halo),
        grid=(slabs, chunks // span),
        in_specs=[
            pl.BlockSpec((rows, channels), lambda s, c: (0, 0)),
            pl.BlockSpec((1, channels, chunk * span), lambda s, c: (s, 0, c)),
            pl.BlockSpec(
                (1, channels, LANES), lambda s, c: (s, 0, jnp.minimum((c + 1) * tiles, last))
            ),
        ],
        out_specs=pl.BlockSpec((parts, rows, chunk + halo), lambda s, c: (0, 0, 0)),
        out_shape=jax.ShapeDtypeStruct((parts, rows, chunk + halo), bf16),
        scratch_shapes=[pltpu.VMEM((DL * rows, channels), bf16)],
        compiler_params=pltpu.CompilerParams(vmem_limit_bytes=VMEM_BYTES),
        name="level0",
    )(channel_delay.T, samples, samples)


def tree_kernel(levels, keep, low_ref, high_ref, amount_ref, dest_ref, *refs):
    x_refs, (out_ref, a_ref, b_ref, o_ref) = refs[:-4], refs[-4:]
    extent = x_refs[0].shape[1]
    rows = out_ref.shape[1]
    trials = low_ref.shape[1]
    cut = rows // len(x_refs)

    def stage(k, carry):
        for half, x_ref in enumerate(x_refs):
            for g in range(0, cut, GROUP):
                x = x_ref[pl.ds(pl.multiple_of(k * cut, GROUP) + g, GROUP), :].astype(f32)
                first = (k * rows + half * cut + g) * SUBLANES
                for j in range(SUBLANES):
                    if j * LANES < extent:
                        piece = x[:, j * LANES : (j + 1) * LANES]
                    else:
                        piece = jnp.zeros((GROUP, LANES), f32)
                    a_ref[pl.ds(first + j, GROUP, stride=SUBLANES), :] = piece
        return carry

    lax.fori_loop(0, trials // rows, stage, 0)
    lane = lax.broadcasted_iota(jnp.int32, (SUBLANES, LANES), 1)
    for level in range(levels):
        src, dst = (a_ref, b_ref) if level % 2 == 0 else (b_ref, a_ref)

        def merge(g, carry):
            for i in range(UNROLL):
                q = g * UNROLL + i
                low = pl.multiple_of(low_ref[level, q], SUBLANES)
                high = pl.multiple_of(high_ref[level, q], SUBLANES)
                amount = amount_ref[level, q]
                v_low = src[pl.ds(low, SUBLANES), :]
                v_high = src[pl.ds(high, SUBLANES), :]
                turned = pltpu.roll(v_high, amount, 1)
                after = pltpu.roll(turned, SUBLANES - 1, 0)
                moved = jnp.where(lane < amount, turned, after)
                value = ((v_low + moved) * half_root).astype(bf16).astype(f32)
                if level + 1 < levels:
                    dst[pl.ds(pl.multiple_of(q * SUBLANES, SUBLANES), SUBLANES), :] = value
                else:
                    o_ref[pl.ds(dest_ref[q], keep, stride=rows), :] = value[:keep]
            return carry

        lax.fori_loop(0, trials // UNROLL, merge, 0)

    def pack(g, carry):
        out_ref[g] = o_ref[pl.ds(pl.multiple_of(g * rows, rows), rows), :].astype(bf16)
        return carry

    lax.fori_loop(0, out_ref.shape[0], pack, 0)


def tree(low, high, amount, places, arrived, keep, rows):
    levels = low.shape[0]
    trials = low.shape[1]
    blocks = trials // rows * keep
    whole = pl.BlockSpec(memory_space=pltpu.VMEM)
    scalars = pl.BlockSpec(memory_space=pltpu.SMEM)
    return pl.pallas_call(
        functools.partial(tree_kernel, levels, keep),
        in_specs=[scalars] * 4 + [whole] * len(arrived),
        out_specs=whole,
        out_shape=jax.ShapeDtypeStruct((blocks, rows, LANES), bf16),
        scratch_shapes=[
            pltpu.VMEM((trials * SUBLANES, LANES), f32),
            pltpu.VMEM((trials * SUBLANES, LANES), f32),
            pltpu.VMEM((blocks * rows, LANES), f32),
        ],
        compiler_params=pltpu.CompilerParams(vmem_limit_bytes=VMEM_BYTES),
        name="tree",
    )(low, high, amount, places, *arrived)


def boxcar_kernel(valid, pitch, widths_ref, scales_ref, x_ref, out_ref, p_ref, t_ref):
    blocks, rows, _ = x_ref.shape
    slabs = out_ref.shape[1]
    per_slab = blocks // slabs
    row = lax.broadcasted_iota(jnp.int32, (LANES, 2 * LANES), 0)
    col = lax.broadcasted_iota(jnp.int32, (LANES, 2 * LANES), 1)
    sums = jnp.where(row < col, 1.0, 0.0).astype(bf16)

    for i in range(valid + 1):
        for s in range(slabs):
            y = jnp.dot(x_ref[s * per_slab + i], sums, preferred_element_type=f32)
            p_ref[pl.ds(i * slabs + s, rows, stride=pitch), :] = y[:, :LANES]
            t_ref[pl.ds(i * slabs + s, rows, stride=pitch), :] = y[:, LANES:]
    lane = lax.broadcasted_iota(jnp.int32, (SUBLANES, LANES), 1)

    def window(g, carry):
        for i in range(4):
            p = g * 4 + i
            scale = scales_ref[p]
            amount = LANES - widths_ref[p]
            base = pl.multiple_of(p * pitch, SUBLANES)
            for b in range(0, valid * slabs, SUBLANES):
                here = p_ref[pl.ds(base + b, SUBLANES), :]
                after = p_ref[pl.ds(base + b + slabs, SUBLANES), :]
                whole = t_ref[pl.ds(base + b, SUBLANES), :]
                end = jnp.where(
                    lane < amount,
                    pltpu.roll(here, amount, 1),
                    pltpu.roll(after, amount, 1) + whole,
                )
                value = (end - here) * scale
                for j in range(0, min(SUBLANES, valid * slabs - b), slabs):
                    t = (b + j) // slabs
                    out_ref[p, :, t * LANES : (t + 1) * LANES] = value[j : j + slabs]
        return carry

    lax.fori_loop(0, rows // 4, window, 0)


def boxcar(widths, arrived, slabs, valid):
    rows = arrived.shape[1]
    pitch = -(-(valid + 1) * slabs // SUBLANES) * SUBLANES + SUBLANES
    whole = pl.BlockSpec(memory_space=pltpu.VMEM)
    scalars = pl.BlockSpec(memory_space=pltpu.SMEM)
    return pl.pallas_call(
        functools.partial(boxcar_kernel, valid, pitch),
        in_specs=[scalars, scalars, whole],
        out_specs=whole,
        out_shape=jax.ShapeDtypeStruct((rows, slabs, valid * LANES), f32),
        scratch_shapes=[
            pltpu.VMEM((rows * pitch, LANES), f32),
            pltpu.VMEM((rows * pitch, LANES), f32),
        ],
        compiler_params=pltpu.CompilerParams(vmem_limit_bytes=VMEM_BYTES),
        name="boxcar",
    )(widths, 1.0 / jnp.sqrt(widths.astype(f32)), arrived)


def exchange_kernel(parts, count, *refs):
    sources, targets = refs[:count], refs[count : 2 * count]
    send_sem, recv_sem, own_sem = refs[2 * count :]
    me = lax.axis_index("band")
    barrier = pltpu.get_barrier_semaphore()
    for k in range(1, parts):
        pl.semaphore_signal(barrier, inc=1, device_id={"band": me ^ k})
    own = [
        pltpu.make_async_copy(sources[a].at[me], targets[a].at[me], own_sem.at[a])
        for a in range(count)
    ]
    for copy in own:
        copy.start()
    pl.semaphore_wait(barrier, parts - 1)
    copies = []
    for k in range(1, parts):
        for a in range(count):
            copies.append(
                pltpu.make_async_remote_copy(
                    src_ref=sources[a].at[me ^ k],
                    dst_ref=targets[a].at[me],
                    send_sem=send_sem.at[a, k],
                    recv_sem=recv_sem.at[a, k],
                    device_id={"band": me ^ k},
                )
            )
            copies[-1].start()
    for copy in own:
        copy.wait()
    for copy in copies:
        copy.wait()


def exchange(arrays, collective_id):
    parts = arrays[0].shape[0]
    count = len(arrays)
    anywhere = pl.BlockSpec(memory_space=pl.ANY)
    return pl.pallas_call(
        functools.partial(exchange_kernel, parts, count),
        in_specs=[anywhere] * count,
        out_specs=[anywhere] * count,
        out_shape=[jax.ShapeDtypeStruct(a.shape, a.dtype) for a in arrays],
        scratch_shapes=[
            pltpu.SemaphoreType.DMA((count, parts)),
            pltpu.SemaphoreType.DMA((count, parts)),
            pltpu.SemaphoreType.DMA((count,)),
        ],
        compiler_params=pltpu.CompilerParams(collective_id=collective_id, has_side_effects=True),
        name="exchange",
    )(*arrays)


def body(samples, channel_delay, merge_rows, merge_shift, destination, widths):
    slabs, length = samples.shape[1], samples.shape[2]
    rows = channel_delay.shape[1]
    parts = lax.axis_size("band")
    levels = merge_shift.shape[0]
    position = lax.axis_index("band")
    chunk = slabs * length // parts
    keep = chunk // LANES
    halo = -(-levels * (DM - 1) // LANES) * LANES

    bits = (2 ** jnp.arange(levels, dtype=jnp.int32))[:, None]
    low = (position & ~bits) * rows + merge_rows[:, 0]
    high = (position | bits) * rows + merge_rows[:, 1]
    owner, slot = destination // rows, destination % rows
    place = owner * (keep * rows) + slot
    tables = jnp.concatenate([low, high, merge_shift, place[None]], axis=0)
    tables = jnp.broadcast_to(tables[None], (parts,) + tables.shape)
    by_slab = jnp.transpose(samples, (1, 0, 2))
    outgoing = level0(by_slab, channel_delay, parts, halo)
    block, tables = exchange([outgoing, tables], 0)
    arrived = [block.reshape(parts * rows, chunk + halo)]
    tables = jnp.transpose(tables, (1, 0, 2)).reshape(tables.shape[1], parts * rows)
    low = tables[:levels] * SUBLANES
    high = tables[levels : 2 * levels] * SUBLANES
    amount = LANES - tables[2 * levels : 3 * levels]
    places = tables[3 * levels]
    merged = tree(low, high, amount, places, arrived, keep, rows)
    grouped = lax.all_to_all(merged, "band", split_axis=0, concat_axis=0, tiled=True)
    valid = (length - MARGIN) // LANES
    return boxcar(widths, grouped, slabs, valid)


def solution(mesh):
    return jax.shard_map(
        body,
        mesh=mesh,
        in_specs=(
            P(("group", "band"), None, None),
            P("band", None),
            P(None, None, "band"),
            P(None, "band"),
            P("band"),
            P("band"),
        ),
        out_specs=P(("group", "band"), None, None),
        check_vma=False,
    )
```
